32 devices in a mesh: leaf: 8 (over z, x), col: 4 (over y, core).
Axes of the slice: x: 2, y: 2, z: 4, core: 2. Of those that a mesh axis runs over, the one named last changes fastest.
Arguments:
- right_side: bfloat16 [16384, 256], P('leaf'), may hold values from -6 to 6
- x_blocks: bfloat16 [8, 4, 96, 128, 128], P('leaf', 'col'), may hold values from -0.109375 to 0.109375
- row_ids: int32 [8, 4, 96], P('leaf', 'col'), may hold values from 0 to 15
- col_ids: int32 [8, 4, 96], P('leaf', 'col'), may hold values from 0 to 7
- counts: int32 [8, 4], P('leaf', 'col'), may hold values from 48 to 96, as said below
Outputs:
- solution: bfloat16 [16384, 256], P(('leaf', 'col'))
The draws below stay inside these ranges and needn't reach their ends.
Inputs may be any that keep to these rules, and one draw needn't show every extreme that they name: `row_ids`: block rows index the rows of the device's own subtree. `col_ids`: slots below 2 are the subtree's own columns; slot 2 + (l - 1) * 2 + s is column s of the level-l separator. `counts`: some device uses all 96 slots; slots past a device's count are unused.
All inputs are finite; a program needn't handle non-finite values.
Results may differ from the reference program's by a relative error of at most 0.0047.
Values may be sent and summed in bfloat16 or wider, within the bound.
No kernel may reach another device: no remote copies, remote signals or barrier semaphores. Data moves between devices by JAX's collectives and lax.ppermute only.
A program may use at most 128 MiB of HBM per device.

```python
import jax
import jax.numpy as jnp
from jax import lax

BLOCK = 128
K = 256
RB_DEV = 16
NBLK = 96
CI = 2
SEP = 2
LEVELS = 3
CT = 8
ORDER = 16384
N_LEAF = 8
N_COL = 4


def draw_counts(key, part):
    first_key = jax.random.fold_in(key, 11)
    second_key = jax.random.fold_in(key, 12)
    third_key = jax.random.fold_in(key, 13)
    values = jax.random.randint(first_key, (N_LEAF * N_COL,), NBLK // 2, NBLK + 1)
    fullest = jax.random.randint(second_key, (), 0, N_LEAF * N_COL)
    emptiest = (fullest + 1 + jax.random.randint(third_key, (), 0, N_LEAF * N_COL - 1)) % (N_LEAF * N_COL)
    positions = jnp.arange(N_LEAF * N_COL)
    values = jnp.where(positions == fullest, NBLK, values)
    values = jnp.where(positions == emptiest, NBLK // 2, values)
    return values.reshape(N_LEAF, N_COL).astype(jnp.int32)


def plant(array, own_key, least, top_value):
    longest = array.shape.index(max(array.shape))
    spots = []
    for shift in (0, 1):
        where = [jax.random.randint(jax.random.fold_in(own_key, axis), (), 0, length) for axis, length in enumerate(array.shape)]
        where[longest] = (where[longest] + shift) % array.shape[longest]
        spots.append(tuple(where))
    return array.at[spots[0]].set(least).at[spots[1]].set(top_value)


def shard_levels(rng, dims, cuts, smallest, largest):
    factor_of, own = 1.0, jax.random.fold_in(rng, 6)
    for axis_at, parts in cuts:
        draws = jnp.exp(jax.random.uniform(jax.random.fold_in(own, axis_at), (parts,), jnp.float32, smallest / len(cuts), largest / len(cuts)))
        factor_of = factor_of * jnp.repeat(draws, dims[axis_at] // parts).reshape([-1 if axis == axis_at else 1 for axis in range(len(dims))])
    return factor_of


def bell_draw(rng, extent, width, most, shards=(), kind=jnp.bfloat16):
    array = jax.random.normal(rng, extent, jnp.float32) * width
    if len(shards) > 0:
        array = shard_levels(rng, extent, shards, -0.22, 0.18) * array
    return jnp.clip(array, min=-most, max=most).astype(kind)


def setup_inputs(seed: int = 0) -> dict:
    splits = jax.random.split(jax.random.key(seed), 6)
    return {
        "right_side": bell_draw(splits[0], (ORDER, K), 1.0, 6.0, ((0, 8),)),
        "x_blocks": bell_draw(splits[1], (N_LEAF, N_COL, NBLK, BLOCK, BLOCK), (BLOCK * NBLK // 4) ** -0.5, 0.109375, ((0, 8), (1, 4))),
        "row_ids": plant(jax.random.randint(splits[2], (N_LEAF, N_COL, NBLK), 0, RB_DEV), jax.random.fold_in(splits[2], 1), 0, RB_DEV - 1).astype(jnp.int32),
        "col_ids": plant(jax.random.randint(splits[3], (N_LEAF, N_COL, NBLK), 0, CT), jax.random.fold_in(splits[3], 1), 0, CT - 1).astype(jnp.int32),
        "counts": draw_counts(jax.random.fold_in(splits[5], 71), 0),
    }


def reference(right_side, x_blocks, row_ids, col_ids, counts):
    num_leaf, num_col, list_len, block_size, _ = x_blocks.shape
    columns = right_side.shape[1]
    rhs_blocks = right_side.reshape(num_leaf, RB_DEV, block_size, columns)
    slot_ids = jnp.arange(list_len, dtype=jnp.int32)
    alive_mask = slot_ids[None, None, :] < counts[:, :, None]
    flat_blocks = x_blocks.reshape(num_leaf * num_col, list_len, block_size, block_size)
    flat_rows = row_ids.reshape(num_leaf * num_col, list_len)
    flat_cols = col_ids.reshape(num_leaf * num_col, list_len)
    flat_alive = alive_mask.reshape(num_leaf * num_col, list_len)
    device_ids = jnp.arange(num_leaf * num_col, dtype=jnp.int32)
    high = lax.Precision.HIGHEST

    def local_partial(items):
        blocks, block_rows, block_cols, alive, device = items
        mine = rhs_blocks[device // num_col]
        picked = mine[block_rows].astype(jnp.float32)
        products = jnp.einsum("kab,kac->kbc", blocks.astype(jnp.float32), picked, precision=high)
        col_select = ((block_cols[None, :] == jnp.arange(CT, dtype=jnp.int32)[:, None]) & alive[None, :]).astype(jnp.float32)
        return jnp.einsum("ck,kbd->cbd", col_select, products, precision=high)

    partial_value = lax.map(local_partial, (flat_blocks, flat_rows, flat_cols, flat_alive, device_ids))
    partial_value = partial_value.reshape(num_leaf, num_col, CT, block_size, columns)
    pieces = [partial_value[:, :, :CI]]
    for level in range(1, LEVELS + 1):
        group = 2 ** level
        segment = partial_value[:, :, CI + (level - 1) * SEP: CI + level * SEP]
        segment = segment.reshape(num_leaf // group, group, num_col, SEP, block_size, columns)
        summed = jnp.sum(segment, axis=1, keepdims=True)
        summed = jnp.broadcast_to(summed, segment.shape).reshape(num_leaf, num_col, SEP, block_size, columns)
        pieces.append(summed)
    combined = jnp.concatenate(pieces, axis=2)
    coarse = combined.astype(jnp.bfloat16).reshape(num_leaf * num_col, CT, block_size, columns)

    def local_terms(items):
        blocks, block_rows, block_cols, alive, coarse_dev = items
        gathered = coarse_dev[block_cols].astype(jnp.float32)
        image = jnp.einsum("kab,kbc->kac", blocks.astype(jnp.float32), gathered, precision=high)
        row_select = ((block_rows[None, :] == jnp.arange(RB_DEV, dtype=jnp.int32)[:, None]) & alive[None, :]).astype(jnp.float32)
        return jnp.einsum("rk,kac->rac", row_select, image, precision=high)

    terms = lax.map(local_terms, (flat_blocks, flat_rows, flat_cols, flat_alive, coarse))
    terms = terms.reshape(num_leaf, num_col, RB_DEV, block_size, columns)
    total = jnp.sum(terms, axis=1)
    return total.reshape(num_leaf * RB_DEV * block_size, columns).astype(jnp.bfloat16)
```

```python
import jax
import jax.numpy as jnp
from jax import lax
from jax.experimental import pallas as pl
from jax.experimental.pallas import tpu as pltpu
from jax.sharding import PartitionSpec as P

CI = 2
SEP = 2
UNROLL = 4
VMEM_LIMIT = 48 << 20


def swap(x, axis, bit):
    return lax.ppermute(x, axis, [(i, i ^ bit) for i in range(lax.axis_size(axis))])


def over_slots(count, list_len, one):
    def group(j, carry):
        for u in range(UNROLL):
            slot = j * UNROLL + u
            one(jnp.minimum(slot, list_len - 1), slot < count)
        return carry

    lax.fori_loop(0, (count + UNROLL - 1) // UNROLL, group, 0)


def gather_kernel(rhs_ref, x_ref, row_ref, col_ref, count_ref, part_ref, half_ref, acc_ref):
    list_len, block, _ = x_ref.shape
    slots = part_ref.shape[0]
    acc_ref[...] = jnp.zeros_like(acc_ref)

    def one(k, used):
        row = pl.multiple_of(row_ref[k] * block, block)
        col = jnp.where(used, col_ref[k], slots)
        acc_ref[col] += lax.dot_general(
            x_ref[k], rhs_ref[pl.ds(row, block), :], (((0,), (0,)), ((), ())), preferred_element_type=jnp.float32
        )

    over_slots(count_ref[0], list_len, one)
    for c in range(slots):
        part_ref[c] = acc_ref[c]
        half_ref[c] = acc_ref[c].astype(jnp.bfloat16)


def image_kernel(coarse_ref, x_ref, row_ref, col_ref, count_ref, side_ref, keep_ref, send_ref, acc_ref):
    list_len, block, _ = x_ref.shape
    groups, per = keep_ref.shape[:2]
    rows = 2 * groups * per
    acc_ref[...] = jnp.zeros_like(acc_ref)

    def one(k, used):
        row = jnp.where(used, row_ref[k], rows)
        acc_ref[row] += jnp.dot(x_ref[k], coarse_ref[col_ref[k]], preferred_element_type=jnp.float32)

    over_slots(count_ref[0], list_len, one)
    side = side_ref[0]
    for g in range(groups):
        for b in range(per):
            keep_ref[g, b] = acc_ref[(2 * g + side) * per + b]
            send_ref[g, b] = acc_ref[(2 * g + 1 - side) * per + b].astype(jnp.bfloat16)


def body(right_side, x_blocks, row_ids, col_ids, counts):
    blocks, block_rows, block_cols, count = x_blocks[0, 0], row_ids[0, 0], col_ids[0, 0], counts[0]
    block = blocks.shape[1]
    columns = right_side.shape[1]
    row_blocks = right_side.shape[0] // block
    levels = lax.axis_size("leaf").bit_length() - 1
    n_col = lax.axis_size("col")
    slots = CI + levels * SEP
    vmem = pl.BlockSpec(memory_space=pltpu.VMEM)
    smem = pl.BlockSpec(memory_space=pltpu.SMEM)
    params = pltpu.CompilerParams(vmem_limit_bytes=VMEM_LIMIT)

    part, half = pl.pallas_call(
        gather_kernel,
        out_shape=(
            jax.ShapeDtypeStruct((slots, block, columns), jnp.float32),
            jax.ShapeDtypeStruct((slots, block, columns), jnp.bfloat16),
        ),
        in_specs=[vmem, vmem, smem, smem, smem],
        out_specs=(vmem, vmem),
        scratch_shapes=[pltpu.VMEM((slots + 1, block, columns), jnp.float32)],
        compiler_params=params,
    )(right_side, blocks, block_rows, block_cols, count)

    done = [half[:CI]]
    own, sent = part[CI:], half[CI:]
    for level in range(levels):
        own = own + swap(sent, "leaf", 1 << level).astype(jnp.float32)
        both = own.astype(jnp.bfloat16)
        done.append(both[:SEP])
        own, sent = own[SEP:], both[SEP:]
    coarse = jnp.concatenate(done, axis=0)

    per = row_blocks // n_col
    side = (lax.axis_index("col") % 2).astype(jnp.int32)
    keep, send = pl.pallas_call(
        image_kernel,
        out_shape=(
            jax.ShapeDtypeStruct((n_col // 2, per, block, columns), jnp.float32),
            jax.ShapeDtypeStruct((n_col // 2, per, block, columns), jnp.bfloat16),
        ),
        in_specs=[vmem, vmem, smem, smem, smem, smem],
        out_specs=(vmem, vmem),
        scratch_shapes=[pltpu.VMEM((row_blocks + 1, block, columns), jnp.float32)],
        compiler_params=params,
    )(coarse, blocks, block_rows, block_cols, count, side[None])

    keep = keep + swap(send, "col", 1).astype(jnp.float32)
    bit = 2
    while bit < n_col:
        side = lax.axis_index("col") // bit % 2
        pairs = keep.reshape(-1, 2, per, block, columns)
        mine = lax.dynamic_index_in_dim(pairs, side, 1, keepdims=False)
        theirs = lax.dynamic_index_in_dim(pairs, 1 - side, 1, keepdims=False)
        keep = mine + swap(theirs.astype(jnp.bfloat16), "col", bit).astype(jnp.float32)
        bit *= 2
    return keep.reshape(per * block, columns).astype(jnp.bfloat16)


def solution(mesh):
    in_specs = (
        P("leaf", None),
        P("leaf", "col", None, None, None),
        P("leaf", "col", None),
        P("leaf", "col", None),
        P("leaf", "col"),
    )
    out_specs = P(("leaf", "col"), None)
    return jax.shard_map(body, mesh=mesh, in_specs=in_specs, out_specs=out_specs, check_vma=False)
```

```python
import functools

import jax
import jax.numpy as jnp
from jax import lax
from jax.experimental import pallas as pl
from jax.experimental.pallas import tpu as pltpu
from jax.sharding import PartitionSpec as P

CI = 2
SEP = 2
BODIES = (24, 8)
CHUNKS = 4
BITS = 10
VMEM_LIMIT = 8 << 20

F32 = jnp.float32
BF16 = jnp.bfloat16
VMEM = pl.BlockSpec(memory_space=pltpu.VMEM)
ANY = pl.BlockSpec(memory_space=pl.ANY)
TOP, REST, FOUND = 0, 1, 2


def swap(x, axis, bits):
    return lax.ppermute(x, axis, [(i, i ^ bits) for i in range(lax.axis_size(axis))])


def over_list(plan_ref, which, one):
    found = plan_ref[FOUND, which]
    mask = (1 << BITS) - 1

    def body(size):
        def group(j, base):
            for u in range(size):
                at = base + u
                entry = plan_ref[which, jnp.minimum(at, found - 1)]
                one(entry & mask, (entry >> BITS) & mask, entry >> (2 * BITS), at < found)
            return base + size

        return group

    base = jnp.int32(0)
    for size in BODIES[:-1]:
        base = lax.fori_loop(0, (found - base) // size, body(size), base)
    size = BODIES[-1]
    lax.fori_loop(0, (found - base + size - 1) // size, body(size), base)


def project(which, low, plan_ref, x_ref, rhs_ref, acc_ref):
    block = x_ref.shape[1]
    trash = acc_ref.shape[0] - 1

    def one(k, row, col, used):
        at = pl.multiple_of(row * block, block)
        acc_ref[jnp.where(used, col - low, trash)] += lax.dot_general(
            x_ref[k], rhs_ref[pl.ds(at, block), :], (((0,), (0,)), ((), ())), preferred_element_type=F32
        )

    over_list(plan_ref, which, one)


def image(which, low, per, flip, plan_ref, x_ref, coarse_ref, acc_ref):
    trash = acc_ref.shape[0] - 1

    def one(k, row, col, used):
        at = ((row // per) ^ flip) * per + row % per
        acc_ref[jnp.where(used, at, trash)] += jnp.dot(x_ref[k], coarse_ref[col - low], preferred_element_type=F32)

    over_list(plan_ref, which, one)


def first_kernel(low, x_hbm, rhs_hbm, row_hbm, col_hbm, count_hbm, x_ref, rhs_ref, part_ref, half_ref, plan_out,
                 row_ref, col_ref, count_ref, plan_ref, acc_ref, id_sem, big_sem):
    list_len = x_ref.shape[0]
    per = list_len // CHUNKS
    ids = [
        pltpu.make_async_copy(row_hbm, row_ref, id_sem.at[0]),
        pltpu.make_async_copy(col_hbm, col_ref, id_sem.at[1]),
        pltpu.make_async_copy(count_hbm, count_ref, id_sem.at[2]),
    ]
    big = [
        pltpu.make_async_copy(x_hbm.at[pl.ds(i * per, per)], x_ref.at[pl.ds(i * per, per)], big_sem.at[i])
        for i in range(CHUNKS)
    ]
    big.append(pltpu.make_async_copy(rhs_hbm, rhs_ref, big_sem.at[CHUNKS]))
    for copy in ids + big:
        copy.start()
    acc_ref[...] = jnp.zeros_like(acc_ref)
    for copy in ids:
        copy.wait()

    def scan(j, found):
        top, rest = found
        for u in range(8):
            k = j * 8 + u
            col = col_ref[k]
            entry = k + (row_ref[k] << BITS) + (col << (2 * BITS))
            used = k < count_ref[0]
            plan_ref[TOP, top] = entry
            plan_ref[REST, rest] = entry
            top += (used & (col >= low)).astype(jnp.int32)
            rest += (used & (col < low)).astype(jnp.int32)
        return top, rest

    top, rest = lax.fori_loop(0, list_len // 8, scan, (jnp.int32(0), jnp.int32(0)))
    plan_ref[FOUND, TOP] = top
    plan_ref[FOUND, REST] = rest
    out = pltpu.make_async_copy(plan_ref, plan_out, id_sem.at[3])
    out.start()
    for copy in big:
        copy.wait()
    project(TOP, low, plan_ref, x_ref, rhs_ref, acc_ref)
    for c in range(part_ref.shape[0]):
        part_ref[c] = acc_ref[c]
        half_ref[c] = acc_ref[c].astype(BF16)
    out.wait()


def rest_kernel(plan_hbm, x_ref, rhs_ref, _, inner_ref, *refs):
    outs, (plan_ref, acc_ref, sem) = refs[:-3], refs[-3:]
    copy = pltpu.make_async_copy(plan_hbm, plan_ref, sem)
    copy.start()
    acc_ref[...] = jnp.zeros_like(acc_ref)
    copy.wait()
    project(REST, 0, plan_ref, x_ref, rhs_ref, acc_ref)
    for c in range(CI):
        inner_ref[c] = acc_ref[c].astype(BF16)
    for n in range(len(outs) // 2):
        part_ref, half_ref = outs[2 * n : 2 * n + 2]
        for c in range(SEP):
            part_ref[c] = acc_ref[CI + n * SEP + c]
            half_ref[c] = acc_ref[CI + n * SEP + c].astype(BF16)


def add_kernel(own_ref, got_ref, *refs):
    sum_ref, half_ref = refs[-2:]
    total = own_ref[...] + got_ref[...].astype(F32)
    sum_ref[...] = total
    half_ref[...] = total.astype(BF16)


def mid_kernel(per, plan_hbm, x_ref, inner_ref, *refs):
    sums, (acc_ref, plan_ref, coarse_ref, sem) = refs[:-5], refs[-4:]
    copy = pltpu.make_async_copy(plan_hbm, plan_ref, sem)
    copy.start()
    acc_ref[...] = jnp.zeros_like(acc_ref)
    coarse_ref[:CI] = inner_ref[...]
    for n in range(len(sums) // 2):
        own_ref, got_ref = sums[2 * n : 2 * n + 2]
        coarse_ref[CI + n * SEP : CI + (n + 1) * SEP] = (own_ref[...] + got_ref[...].astype(F32)).astype(BF16)
    copy.wait()
    image(REST, 0, per, lax.axis_index("col"), plan_ref, x_ref, coarse_ref, acc_ref)


def last_kernel(low, per, plan_hbm, x_ref, own_ref, got_ref, old_ref, acc_ref, keep_ref, send_ref, plan_ref, coarse_ref, sem):
    copy = pltpu.make_async_copy(plan_hbm, plan_ref, sem)
    copy.start()
    coarse_ref[...] = (own_ref[...] + got_ref[...].astype(F32)).astype(BF16)
    copy.wait()
    image(TOP, low, per, lax.axis_index("col"), plan_ref, x_ref, coarse_ref, acc_ref)
    for g in range(keep_ref.shape[0]):
        for b in range(per):
            send_ref[g, b] = acc_ref[(2 * g + 1) * per + b].astype(BF16)
            keep_ref[g, b] = acc_ref[2 * g * per + b]


def body(right_side, x_blocks, row_ids, col_ids, counts):
    blocks, rows, cols, count = x_blocks[0, 0], row_ids[0, 0], col_ids[0, 0], counts[0]
    list_len, block, _ = blocks.shape
    columns = right_side.shape[1]
    row_blocks = right_side.shape[0] // block
    levels = lax.axis_size("leaf").bit_length() - 1
    n_col = lax.axis_size("col")
    per = row_blocks // n_col
    slots = CI + levels * SEP
    low = slots - SEP
    params = pltpu.CompilerParams(vmem_limit_bytes=VMEM_LIMIT)
    free = pl.CostEstimate(flops=0, bytes_accessed=0, transcendentals=0)

    def tiles(n, dtype):
        return pltpu.VMEM((n, block, columns), dtype)

    def in_vmem(*arrays):
        return [pltpu.with_memory_space_constraint(a, pltpu.VMEM) for a in arrays]

    def in_hbm(*arrays):
        return [pltpu.with_memory_space_constraint(a, pltpu.HBM) for a in arrays]

    plan_shape = (8, (list_len + 128) // 128 * 128)
    plan_scratch = pltpu.SMEM(plan_shape, jnp.int32)
    pair = (tiles(SEP, F32), tiles(SEP, BF16))
    sem = pltpu.SemaphoreType.DMA

    x_vmem, rhs_vmem, part, half, plan = pl.pallas_call(
        functools.partial(first_kernel, low),
        out_shape=(pltpu.VMEM(blocks.shape, BF16), pltpu.VMEM(right_side.shape, BF16), *pair, pltpu.VMEM(plan_shape, jnp.int32)),
        in_specs=[ANY] * 5,
        out_specs=(VMEM,) * 5,
        scratch_shapes=[
            pltpu.SMEM((list_len,), jnp.int32),
            pltpu.SMEM((list_len,), jnp.int32),
            pltpu.SMEM((1,), jnp.int32),
            plan_scratch,
            tiles(SEP + 1, F32),
            sem((4,)),
            sem((CHUNKS + 1,)),
        ],
        compiler_params=params,
        cost_estimate=free,
    )(*in_hbm(blocks, right_side, rows, cols), count)
    own, sent, got = {levels: part}, {levels: half}, {}

    def exchange(level, step):
        bits = (2 << step) - 2 if step > 1 else 1 << step
        got[level] = swap(sent[level], "leaf", bits)

    def add(level, *alive):
        own[level], sent[level] = pl.pallas_call(
            add_kernel,
            out_shape=pair,
            in_specs=[VMEM] * (2 + len(alive)),
            out_specs=(VMEM,) * 2,
            compiler_params=params,
            cost_estimate=free,
        )(*in_vmem(own[level], got[level], *alive))

    inner, *others = pl.pallas_call(
        rest_kernel,
        out_shape=(tiles(CI, BF16), *pair * (levels - 1)),
        in_specs=[VMEM] * 4,
        out_specs=(VMEM,) * (2 * levels - 1),
        scratch_shapes=[plan_scratch, tiles(low + 1, F32), sem(())],
        compiler_params=params,
        cost_estimate=free,
    )(*in_vmem(plan, x_vmem, rhs_vmem, own[levels]))
    for n in range(levels - 1):
        own[n + 1], sent[n + 1] = others[2 * n : 2 * n + 2]

    for step in range(levels):
        for level in range(levels, step, -1):
            exchange(level, step)
            if level > step + 1:
                add(level, x_vmem, inner, *[own[n] for n in range(1, levels) if n != level])

    sums = [array for level in range(1, levels) for array in (own[level], got[level])]
    terms = pl.pallas_call(
        functools.partial(mid_kernel, per),
        out_shape=tiles(row_blocks + 1, F32),
        in_specs=[VMEM] * (4 + len(sums)),
        out_specs=VMEM,
        scratch_shapes=[plan_scratch, tiles(low, BF16), sem(())],
        compiler_params=params,
        cost_estimate=free,
    )(*in_vmem(plan, x_vmem, inner, *sums, own[levels]))

    _, keep, send = pl.pallas_call(
        functools.partial(last_kernel, low, per),
        out_shape=(
            tiles(row_blocks + 1, F32),
            pltpu.VMEM((n_col // 2, per, block, columns), F32),
            pltpu.VMEM((n_col // 2, per, block, columns), BF16),
        ),
        in_specs=[VMEM] * 5,
        out_specs=(VMEM,) * 3,
        scratch_shapes=[plan_scratch, tiles(SEP, BF16), sem(())],
        input_output_aliases={4: 0},
        compiler_params=params,
        cost_estimate=free,
    )(*in_vmem(plan, x_vmem, own[levels], got[levels], terms))

    bit = 1
    while True:
        keep = keep + swap(send, "col", bit).astype(F32)
        bit *= 2
        if bit == n_col:
            return keep.reshape(per * block, columns).astype(BF16)
        pairs = keep.reshape(-1, 2, per, block, columns)
        keep, send = pairs[:, 0], pairs[:, 1].astype(BF16)


def solution(mesh):
    in_specs = (
        P("leaf", None),
        P("leaf", "col", None, None, None),
        P("leaf", "col", None),
        P("leaf", "col", None),
        P("leaf", "col"),
    )
    out_specs = P(("leaf", "col"), None)
    return jax.shard_map(body, mesh=mesh, in_specs=in_specs, out_specs=out_specs, check_vma=False)
```

```python
import functools

import jax
import jax.numpy as jnp
from jax import lax
from jax.experimental import pallas as pl
from jax.experimental.pallas import tpu as pltpu
from jax.sharding import PartitionSpec as P

CI = 2
SEP = 2
LARGE, SMALL = 24, 12
CHUNKS = 4
BITS = 10
VMEM_LIMIT = 8 << 20

F32 = jnp.float32
BF16 = jnp.bfloat16
VMEM = pl.BlockSpec(memory_space=pltpu.VMEM)
SMEM = pl.BlockSpec(memory_space=pltpu.SMEM)
ANY = pl.BlockSpec(memory_space=pl.ANY)
ALL, TOP, REST, FAR, NEAR, SIZES, PLAN_ROWS = 0, 1, 2, 3, 4, 5, 8


def swap(x, axis, bits):
    return lax.ppermute(x, axis, [(i, i ^ bits) for i in range(lax.axis_size(axis))])


def over_list(plan_ref, which, begin, end, one):
    mask = (1 << BITS) - 1

    def body(size):
        def group(j, base):
            for u in range(size):
                at = base + u
                entry = plan_ref[which, jnp.minimum(at, end - 1)]
                one(entry & mask, (entry >> BITS) & mask, entry >> (2 * BITS), at < end)
            return base + size

        return group

    base = lax.fori_loop(0, (end - begin + LARGE - SMALL - 1) // LARGE, body(LARGE), begin)
    lax.fori_loop(0, (end - base + SMALL - 1) // SMALL, body(SMALL), base)


def project(which, begin, end, low, plan_ref, x_ref, rhs_ref, acc_ref):
    block = x_ref.shape[1]
    trash = acc_ref.shape[0] - 1

    def one(k, row, col, used):
        at = pl.multiple_of(row * block, block)
        acc_ref[jnp.where(used, col - low, trash)] += lax.dot_general(
            x_ref[k], rhs_ref[pl.ds(at, block), :], (((0,), (0,)), ((), ())), preferred_element_type=F32
        )

    over_list(plan_ref, which, begin, end, one)


def image(which, begin, end, low, per, flip, plan_ref, x_ref, coarse_ref, acc_ref):
    trash = acc_ref.shape[0] - 1

    def one(k, row, col, used):
        at = ((row // per) ^ flip) * per + row % per
        acc_ref[jnp.where(used, at, trash)] += jnp.dot(x_ref[k], coarse_ref[col - low], preferred_element_type=F32)

    over_list(plan_ref, which, begin, end, one)


def list_slots(plan_ref, found, low, high, list_len):
    def scan(j, found):
        for u in range(8):
            entry = plan_ref[ALL, j * 8 + u]
            plan_ref[REST, found] = entry
            col = entry >> (2 * BITS)
            found += ((col >= low) & (col < high)).astype(jnp.int32)
        return found

    return lax.fori_loop(0, list_len // 8, scan, found)


def first_kernel(low, high, x_hbm, rhs_hbm, row_hbm, col_hbm, count_hbm, x_ref, rhs_ref, part_ref, half_ref, plan_ref,
                 row_ref, col_ref, count_ref, acc_ref, id_sem, big_sem):
    list_len = x_ref.shape[0]
    chunk = list_len // CHUNKS
    ids = [
        pltpu.make_async_copy(row_hbm, row_ref, id_sem.at[0]),
        pltpu.make_async_copy(col_hbm, col_ref, id_sem.at[1]),
        pltpu.make_async_copy(count_hbm, count_ref, id_sem.at[2]),
    ]
    big = [pltpu.make_async_copy(rhs_hbm, rhs_ref, big_sem.at[CHUNKS])]
    for i in range(CHUNKS):
        at = pl.ds(i * chunk, chunk)
        big.append(pltpu.make_async_copy(x_hbm.at[at], x_ref.at[at], big_sem.at[i]))
    for copy in ids + big:
        copy.start()
    acc_ref[...] = jnp.zeros_like(acc_ref)
    for copy in ids:
        copy.wait()
    count = count_ref[0]

    def scan(j, carry):
        found, second = carry
        for u in range(8):
            k = j * 8 + u
            col = jnp.where(k < count, col_ref[k], high)
            entry = k + (row_ref[k] << BITS) + (col << (2 * BITS))
            plan_ref[ALL, k] = entry
            plan_ref[TOP, found] = entry
            plan_ref[REST, second] = entry
            found += ((col >= low) & (col < high)).astype(jnp.int32)
            second += ((col >= low - SEP) & (col < low)).astype(jnp.int32)
        return found, second

    found, second = lax.fori_loop(0, list_len // 8, scan, (jnp.int32(0), jnp.int32(0)))
    plan_ref[SIZES, TOP] = found
    plan_ref[SIZES, REST] = second
    for copy in big:
        copy.wait()
    project(TOP, jnp.int32(0), found, low, plan_ref, x_ref, rhs_ref, acc_ref)
    for c in range(high - low):
        part_ref[c] = acc_ref[c]
        half_ref[c] = acc_ref[c].astype(BF16)


def part_kernel(low, high, second, old_plan_ref, x_ref, rhs_ref, _, plan_ref, *refs):
    outs, acc_ref = refs[:-1], refs[-1]
    acc_ref[...] = jnp.zeros_like(acc_ref)
    begin, end = jnp.int32(0), plan_ref[SIZES, REST]
    if not second:
        begin, end = end, list_slots(plan_ref, end, low, high, x_ref.shape[0])
        plan_ref[SIZES, REST] = end
    project(REST, begin, end, low, plan_ref, x_ref, rhs_ref, acc_ref)
    for n in range(len(outs) // 2):
        part_ref, half_ref = outs[2 * n : 2 * n + 2]
        for c in range(SEP):
            part_ref[c] = acc_ref[n * SEP + c]
            half_ref[c] = acc_ref[n * SEP + c].astype(BF16)


def add_kernel(own_ref, got_ref, *refs):
    sum_ref, half_ref = refs[-2:]
    total = own_ref[...] + got_ref[...].astype(F32)
    sum_ref[...] = total
    half_ref[...] = total.astype(BF16)


def inner_kernel(per, old_plan_ref, x_ref, rhs_ref, *refs):
    acc_ref, plan_ref, part_ref, coarse_ref = refs[-4:]
    part_ref[...] = jnp.zeros_like(part_ref)
    acc_ref[...] = jnp.zeros_like(acc_ref)
    me = lax.axis_index("col")
    half = (acc_ref.shape[0] - 1) // per // 2

    def scan(j, found):
        far, near = found
        entry = plan_ref[TOP, j]
        plan_ref[FAR, far] = entry
        plan_ref[NEAR, near] = entry
        is_far = (((((entry >> BITS) & ((1 << BITS) - 1)) // per) ^ me) >= half).astype(jnp.int32)
        return far + is_far, near + 1 - is_far

    far, near = lax.fori_loop(0, plan_ref[SIZES, TOP], scan, (jnp.int32(0), jnp.int32(0)))
    plan_ref[SIZES, FAR] = far
    plan_ref[SIZES, NEAR] = near
    begin = plan_ref[SIZES, REST]
    end = list_slots(plan_ref, begin, 0, CI, x_ref.shape[0])
    project(REST, begin, end, 0, plan_ref, x_ref, rhs_ref, part_ref)
    coarse_ref[...] = part_ref[:CI].astype(BF16)
    image(REST, begin, end, 0, per, me, plan_ref, x_ref, coarse_ref, acc_ref)


def mid_kernel(per, plan_ref, x_ref, *refs):
    sums, (old_ref, acc_ref, coarse_ref) = refs[:-3], refs[-3:]
    for n in range(len(sums) // 2):
        own_ref, got_ref = sums[2 * n : 2 * n + 2]
        coarse_ref[n * SEP : (n + 1) * SEP] = (own_ref[...] + got_ref[...].astype(F32)).astype(BF16)
    image(REST, jnp.int32(0), plan_ref[SIZES, REST], CI, per, lax.axis_index("col"), plan_ref, x_ref, coarse_ref, acc_ref)


def split(half, per, acc_ref, keep_ref, send_ref):
    for g in range(keep_ref.shape[0]):
        for b in range(per):
            send_ref[g, b] = acc_ref[half + (2 * g + 1) * per + b].astype(BF16)
            keep_ref[g, b] = acc_ref[half + 2 * g * per + b]


def far_kernel(low, per, plan_ref, x_ref, own_ref, got_ref, old_ref, acc_ref, coarse_ref, keep_ref, send_ref):
    coarse_ref[...] = (own_ref[...] + got_ref[...].astype(F32)).astype(BF16)
    image(FAR, jnp.int32(0), plan_ref[SIZES, FAR], low, per, lax.axis_index("col"), plan_ref, x_ref, coarse_ref, acc_ref)
    split((acc_ref.shape[0] - 1) // 2, per, acc_ref, keep_ref, send_ref)


def near_kernel(low, per, plan_ref, x_ref, coarse_ref, old_ref, acc_ref, keep_ref, send_ref):
    image(NEAR, jnp.int32(0), plan_ref[SIZES, NEAR], low, per, lax.axis_index("col"), plan_ref, x_ref, coarse_ref, acc_ref)
    split(0, per, acc_ref, keep_ref, send_ref)


def body(right_side, x_blocks, row_ids, col_ids, counts):
    blocks, rows, cols, count = x_blocks[0, 0], row_ids[0, 0], col_ids[0, 0], counts[0]
    list_len, block, _ = blocks.shape
    columns = right_side.shape[1]
    row_blocks = right_side.shape[0] // block
    levels = lax.axis_size("leaf").bit_length() - 1
    n_col = lax.axis_size("col")
    per = row_blocks // n_col
    slots = CI + levels * SEP
    low = slots - SEP
    params = pltpu.CompilerParams(vmem_limit_bytes=VMEM_LIMIT)
    free = pl.CostEstimate(flops=0, bytes_accessed=0, transcendentals=0)

    def tiles(n, dtype):
        return pltpu.VMEM((n, block, columns), dtype)

    def in_vmem(*arrays):
        return [pltpu.with_memory_space_constraint(a, pltpu.VMEM) for a in arrays]

    def in_hbm(*arrays):
        return [pltpu.with_memory_space_constraint(a, pltpu.HBM) for a in arrays]

    plan_shape = (PLAN_ROWS, (list_len + 128) // 128 * 128)
    plan_out = pltpu.SMEM(plan_shape, jnp.int32)
    pair = (tiles(SEP, F32), tiles(SEP, BF16))
    sem = pltpu.SemaphoreType.DMA

    x_vmem, rhs_vmem, part, half, plan = pl.pallas_call(
        functools.partial(first_kernel, low, slots),
        out_shape=(pltpu.VMEM(blocks.shape, BF16), pltpu.VMEM(right_side.shape, BF16), *pair, plan_out),
        in_specs=[ANY] * 5,
        out_specs=(*(VMEM,) * 4, SMEM),
        scratch_shapes=[
            pltpu.SMEM((list_len,), jnp.int32),
            pltpu.SMEM((list_len,), jnp.int32),
            pltpu.SMEM((1,), jnp.int32),
            tiles(SEP + 1, F32),
            sem((3,)),
            sem((CHUNKS + 1,)),
        ],
        compiler_params=params,
        cost_estimate=free,
    )(*in_hbm(blocks, right_side, rows, cols), count)
    own, sent, got = {levels: part}, {levels: half}, {}

    def exchange(level, step):
        bits = (2 << step) - 2 if step > 1 else 1 << step
        got[level] = swap(sent[level], "leaf", bits)

    def add(level, *alive):
        own[level], sent[level] = pl.pallas_call(
            add_kernel,
            out_shape=pair,
            in_specs=[VMEM] * (2 + len(alive)),
            out_specs=(VMEM,) * 2,
            compiler_params=params,
            cost_estimate=free,
        )(*in_vmem(own[level], got[level], *alive))

    def parts_of(plan, low, high, second, after):
        pairs = pair * ((high - low) // SEP)
        return pl.pallas_call(
            functools.partial(part_kernel, low, high, second),
            out_shape=(plan_out, *pairs),
            in_specs=[SMEM, VMEM, VMEM, VMEM],
            out_specs=(SMEM, *(VMEM,) * len(pairs)),
            scratch_shapes=[tiles(high - low + 1, F32)],
            input_output_aliases={0: 0},
            compiler_params=params,
            cost_estimate=free,
        )(plan, *in_vmem(x_vmem, rhs_vmem, after))

    plan, own[levels - 1], sent[levels - 1] = parts_of(plan, low - SEP, low, True, own[levels])
    for step in range(levels):
        for level in range(levels, step, -1):
            exchange(level, step if level == levels else level - 1 - step)
            if level > step + 1:
                add(level, x_vmem, rhs_vmem, *[array for n, array in own.items() if n != level])
            if (level, step) == (levels, 0):
                plan, *others = parts_of(plan, CI, low - SEP, False, sent[levels])
                for n in range(levels - 2):
                    own[n + 1], sent[n + 1] = others[2 * n : 2 * n + 2]

    terms, plan = pl.pallas_call(
        functools.partial(inner_kernel, per),
        out_shape=(tiles(row_blocks + 1, F32), plan_out),
        in_specs=[SMEM] + [VMEM] * (3 + len(own)),
        out_specs=(VMEM, SMEM),
        scratch_shapes=[tiles(CI + 1, F32), tiles(CI, BF16)],
        input_output_aliases={0: 1},
        compiler_params=params,
        cost_estimate=free,
    )(plan, *in_vmem(x_vmem, rhs_vmem, sent[levels], *own.values()))

    sums = [array for level in range(1, levels) for array in (own[level], got[level])]
    terms = pl.pallas_call(
        functools.partial(mid_kernel, per),
        out_shape=tiles(row_blocks + 1, F32),
        in_specs=[SMEM] + [VMEM] * (2 + len(sums)),
        out_specs=VMEM,
        scratch_shapes=[tiles(low - CI, BF16)],
        input_output_aliases={2 + len(sums): 0},
        compiler_params=params,
        cost_estimate=free,
    )(plan, *in_vmem(x_vmem, *sums, terms))

    part_shape = (n_col // 4, per, block, columns)
    parts = (pltpu.VMEM(part_shape, F32), pltpu.VMEM(part_shape, BF16))
    terms, coarse, far, far_send = pl.pallas_call(
        functools.partial(far_kernel, low, per),
        out_shape=(tiles(row_blocks + 1, F32), tiles(SEP, BF16), *parts),
        in_specs=[SMEM] + [VMEM] * 4,
        out_specs=(VMEM,) * 4,
        input_output_aliases={4: 0},
        compiler_params=params,
        cost_estimate=free,
    )(plan, *in_vmem(x_vmem, own[levels], got[levels], terms))
    _, near, near_send = pl.pallas_call(
        functools.partial(near_kernel, low, per),
        out_shape=(tiles(row_blocks + 1, F32), *parts),
        in_specs=[SMEM] + [VMEM] * 3,
        out_specs=(VMEM,) * 3,
        input_output_aliases={3: 0},
        compiler_params=params,
        cost_estimate=free,
    )(plan, *in_vmem(x_vmem, coarse, terms))

    def reduce_low_bits(keep, send):
        bit = 1
        while True:
            keep = keep + swap(send, "col", bit).astype(F32)
            bit *= 2
            if bit == n_col // 2:
                return keep[0]
            pairs = keep.reshape(-1, 2, per, block, columns)
            keep, send = pairs[:, 0], pairs[:, 1].astype(BF16)

    far = reduce_low_bits(far, far_send).astype(BF16)
    total = reduce_low_bits(near, near_send) + swap(far, "col", n_col // 2).astype(F32)
    return total.reshape(per * block, columns).astype(BF16)


def solution(mesh):
    in_specs = (
        P("leaf", None),
        P("leaf", "col", None, None, None),
        P("leaf", "col", None),
        P("leaf", "col", None),
        P("leaf", "col"),
    )
    out_specs = P(("leaf", "col"), None)
    return jax.shard_map(body, mesh=mesh, in_specs=in_specs, out_specs=out_specs, check_vma=False)
```

```python
import functools

import jax
import jax.numpy as jnp
from jax import lax
from jax.experimental import pallas as pl
from jax.experimental.pallas import tpu as pltpu
from jax.sharding import PartitionSpec as P

CI = 2
SEP = 2
LARGE, SMALL = 24, 12
CHUNKS = 4
BITS = 10
VMEM_LIMIT = 8 << 20

F32 = jnp.float32
BF16 = jnp.bfloat16
VMEM = pl.BlockSpec(memory_space=pltpu.VMEM)
SMEM = pl.BlockSpec(memory_space=pltpu.SMEM)
ANY = pl.BlockSpec(memory_space=pl.ANY)
ALL, TOP, REST, FAR, NEAR, SIZES, PLAN_ROWS = 0, 1, 2, 3, 4, 5, 8


def swap(x, axis, bits):
    return lax.ppermute(x, axis, [(i, i ^ bits) for i in range(lax.axis_size(axis))])


def over_list(plan_ref, which, begin, end, one):
    mask = (1 << BITS) - 1

    def body(size):
        def group(j, base):
            for u in range(size):
                at = base + u
                entry = plan_ref[which, jnp.minimum(at, end - 1)]
                one(entry & mask, (entry >> BITS) & mask, entry >> (2 * BITS), at < end)
            return base + size

        return group

    base = lax.fori_loop(0, (end - begin + LARGE - SMALL - 1) // LARGE, body(LARGE), begin)
    lax.fori_loop(0, (end - base + SMALL - 1) // SMALL, body(SMALL), base)


def project(which, begin, end, low, plan_ref, x_ref, rhs_ref, acc_ref):
    block = x_ref.shape[1]
    trash = acc_ref.shape[0] - 1

    def one(k, row, col, used):
        at = pl.multiple_of(row * block, block)
        acc_ref[jnp.where(used, col - low, trash)] += lax.dot_general(
            x_ref[k], rhs_ref[pl.ds(at, block), :], (((0,), (0,)), ((), ())), preferred_element_type=F32
        )

    over_list(plan_ref, which, begin, end, one)


def image(which, begin, end, low, per, flip, plan_ref, x_ref, coarse_ref, acc_ref):
    trash = acc_ref.shape[0] - 1

    def one(k, row, col, used):
        at = ((row // per) ^ flip) * per + row % per
        acc_ref[jnp.where(used, at, trash)] += jnp.dot(x_ref[k], coarse_ref[col - low], preferred_element_type=F32)

    over_list(plan_ref, which, begin, end, one)


def list_slots(plan_ref, found, low, high, list_len):
    def scan(j, found):
        for u in range(8):
            entry = plan_ref[ALL, j * 8 + u]
            plan_ref[REST, found] = entry
            col = entry >> (2 * BITS)
            found += ((col >= low) & (col < high)).astype(jnp.int32)
        return found

    return lax.fori_loop(0, list_len // 8, scan, found)


def first_kernel(low, high, x_hbm, rhs_hbm, row_hbm, col_hbm, count_hbm, x_ref, rhs_ref, part_ref, half_ref, plan_ref,
                 row_ref, col_ref, count_ref, acc_ref, id_sem, big_sem):
    list_len = x_ref.shape[0]
    chunk = list_len // CHUNKS
    ids = [
        pltpu.make_async_copy(row_hbm, row_ref, id_sem.at[0]),
        pltpu.make_async_copy(col_hbm, col_ref, id_sem.at[1]),
        pltpu.make_async_copy(count_hbm, count_ref, id_sem.at[2]),
    ]
    big = [pltpu.make_async_copy(rhs_hbm, rhs_ref, big_sem.at[CHUNKS])]
    for i in range(CHUNKS):
        at = pl.ds(i * chunk, chunk)
        big.append(pltpu.make_async_copy(x_hbm.at[at], x_ref.at[at], big_sem.at[i]))
    for copy in ids + big:
        copy.start()
    acc_ref[...] = jnp.zeros_like(acc_ref)
    for copy in ids:
        copy.wait()
    count = count_ref[0]

    def scan(j, carry):
        found, second = carry
        for u in range(8):
            k = j * 8 + u
            col = jnp.where(k < count, col_ref[k], high)
            entry = k + (row_ref[k] << BITS) + (col << (2 * BITS))
            plan_ref[ALL, k] = entry
            plan_ref[TOP, found] = entry
            plan_ref[REST, second] = entry
            found += ((col >= low) & (col < high)).astype(jnp.int32)
            second += ((col >= low - SEP) & (col < low)).astype(jnp.int32)
        return found, second

    found, second = lax.fori_loop(0, list_len // 8, scan, (jnp.int32(0), jnp.int32(0)))
    plan_ref[SIZES, TOP] = found
    plan_ref[SIZES, REST] = second
    for copy in big:
        copy.wait()
    project(TOP, jnp.int32(0), found, low, plan_ref, x_ref, rhs_ref, acc_ref)
    for c in range(high - low):
        part_ref[c] = acc_ref[c]
        half_ref[c] = acc_ref[c].astype(BF16)


def part_kernel(low, high, second, old_plan_ref, x_ref, rhs_ref, _, plan_ref, *refs):
    outs, acc_ref = refs[:-1], refs[-1]
    acc_ref[...] = jnp.zeros_like(acc_ref)
    begin, end = jnp.int32(0), plan_ref[SIZES, REST]
    if not second:
        begin = plan_ref[SIZES, ALL] if low == 0 else end
        end = list_slots(plan_ref, begin, low, high, x_ref.shape[0])
        plan_ref[SIZES, ALL] = end
    project(REST, begin, end, low, plan_ref, x_ref, rhs_ref, acc_ref)
    if low == 0:
        for c in range(CI):
            outs[0][c] = acc_ref[c].astype(BF16)
    for n in range(len(outs) // 2):
        part_ref, half_ref = outs[2 * n : 2 * n + 2]
        for c in range(SEP):
            part_ref[c] = acc_ref[n * SEP + c]
            half_ref[c] = acc_ref[n * SEP + c].astype(BF16)


def add_kernel(own_ref, got_ref, *refs):
    sum_ref, half_ref = refs[-2:]
    total = own_ref[...] + got_ref[...].astype(F32)
    sum_ref[...] = total
    half_ref[...] = total.astype(BF16)


def sum_coarse(sums, coarse_ref, at):
    for n in range(len(sums) // 2):
        own_ref, got_ref = sums[2 * n : 2 * n + 2]
        coarse_ref[at + n * SEP : at + (n + 1) * SEP] = (own_ref[...] + got_ref[...].astype(F32)).astype(BF16)


def lower_kernel(per, levels, old_plan_ref, x_ref, inner_ref, *refs):
    acc_ref, plan_ref, coarse_ref = refs[-3:]
    acc_ref[...] = jnp.zeros_like(acc_ref)
    coarse_ref[:CI] = inner_ref[...]
    sum_coarse(refs[: 2 * levels], coarse_ref, CI)
    me = lax.axis_index("col")
    half = (acc_ref.shape[0] - 1) // per // 2

    def scan(j, found):
        far, near = found
        entry = plan_ref[TOP, j]
        plan_ref[FAR, far] = entry
        plan_ref[NEAR, near] = entry
        is_far = (((((entry >> BITS) & ((1 << BITS) - 1)) // per) ^ me) >= half).astype(jnp.int32)
        return far + is_far, near + 1 - is_far

    far, near = lax.fori_loop(0, plan_ref[SIZES, TOP], scan, (jnp.int32(0), jnp.int32(0)))
    plan_ref[SIZES, FAR] = far
    plan_ref[SIZES, NEAR] = near
    image(REST, plan_ref[SIZES, REST], plan_ref[SIZES, ALL], 0, per, me, plan_ref, x_ref, coarse_ref, acc_ref)


def mid_kernel(per, low, plan_ref, x_ref, own_ref, got_ref, old_ref, acc_ref, coarse_ref):
    sum_coarse((own_ref, got_ref), coarse_ref, 0)
    image(REST, jnp.int32(0), plan_ref[SIZES, REST], low, per, lax.axis_index("col"), plan_ref, x_ref, coarse_ref, acc_ref)


def split(half, per, acc_ref, keep_ref, send_ref):
    for g in range(keep_ref.shape[0]):
        for b in range(per):
            send_ref[g, b] = acc_ref[half + (2 * g + 1) * per + b].astype(BF16)
            keep_ref[g, b] = acc_ref[half + 2 * g * per + b]


def far_kernel(low, per, plan_ref, x_ref, own_ref, got_ref, old_ref, acc_ref, coarse_ref, keep_ref, send_ref):
    coarse_ref[...] = (own_ref[...] + got_ref[...].astype(F32)).astype(BF16)
    image(FAR, jnp.int32(0), plan_ref[SIZES, FAR], low, per, lax.axis_index("col"), plan_ref, x_ref, coarse_ref, acc_ref)
    split((acc_ref.shape[0] - 1) // 2, per, acc_ref, keep_ref, send_ref)


def near_kernel(low, per, plan_ref, x_ref, coarse_ref, old_ref, acc_ref, keep_ref, send_ref):
    image(NEAR, jnp.int32(0), plan_ref[SIZES, NEAR], low, per, lax.axis_index("col"), plan_ref, x_ref, coarse_ref, acc_ref)
    split(0, per, acc_ref, keep_ref, send_ref)


def body(right_side, x_blocks, row_ids, col_ids, counts):
    blocks, rows, cols, count = x_blocks[0, 0], row_ids[0, 0], col_ids[0, 0], counts[0]
    list_len, block, _ = blocks.shape
    columns = right_side.shape[1]
    row_blocks = right_side.shape[0] // block
    levels = lax.axis_size("leaf").bit_length() - 1
    n_col = lax.axis_size("col")
    per = row_blocks // n_col
    slots = CI + levels * SEP
    low = slots - SEP
    params = pltpu.CompilerParams(vmem_limit_bytes=VMEM_LIMIT)
    free = pl.CostEstimate(flops=0, bytes_accessed=0, transcendentals=0)

    def tiles(n, dtype):
        return pltpu.VMEM((n, block, columns), dtype)

    def in_vmem(*arrays):
        return [pltpu.with_memory_space_constraint(a, pltpu.VMEM) for a in arrays]

    def in_hbm(*arrays):
        return [pltpu.with_memory_space_constraint(a, pltpu.HBM) for a in arrays]

    plan_shape = (PLAN_ROWS, (list_len + 128) // 128 * 128)
    plan_out = pltpu.SMEM(plan_shape, jnp.int32)
    pair = (tiles(SEP, F32), tiles(SEP, BF16))
    sem = pltpu.SemaphoreType.DMA

    x_vmem, rhs_vmem, part, half, plan = pl.pallas_call(
        functools.partial(first_kernel, low, slots),
        out_shape=(pltpu.VMEM(blocks.shape, BF16), pltpu.VMEM(right_side.shape, BF16), *pair, plan_out),
        in_specs=[ANY] * 5,
        out_specs=(*(VMEM,) * 4, SMEM),
        scratch_shapes=[
            pltpu.SMEM((list_len,), jnp.int32),
            pltpu.SMEM((list_len,), jnp.int32),
            pltpu.SMEM((1,), jnp.int32),
            tiles(SEP + 1, F32),
            sem((3,)),
            sem((CHUNKS + 1,)),
        ],
        compiler_params=params,
        cost_estimate=free,
    )(*in_hbm(blocks, right_side, rows, cols), count)
    own, sent, got = {levels: part}, {levels: half}, {}

    def exchange(level, step):
        bits = (2 << step) - 2 if step > 1 else 1 << step
        got[level] = swap(sent[level], "leaf", bits)

    def add(level, *alive):
        own[level], sent[level] = pl.pallas_call(
            add_kernel,
            out_shape=pair,
            in_specs=[VMEM] * (2 + len(alive)),
            out_specs=(VMEM,) * 2,
            compiler_params=params,
            cost_estimate=free,
        )(*in_vmem(own[level], got[level], *alive))

    def parts_of(plan, low, high, second, after):
        pairs = (tiles(CI, BF16),) if low == 0 else pair * ((high - low) // SEP)
        return pl.pallas_call(
            functools.partial(part_kernel, low, high, second),
            out_shape=(plan_out, *pairs),
            in_specs=[SMEM, VMEM, VMEM, VMEM],
            out_specs=(SMEM, *(VMEM,) * len(pairs)),
            scratch_shapes=[tiles(high - low + 1, F32)],
            input_output_aliases={0: 0},
            compiler_params=params,
            cost_estimate=free,
        )(plan, *in_vmem(x_vmem, rhs_vmem, after))

    plan, own[levels - 1], sent[levels - 1] = parts_of(plan, low - SEP, low, True, own[levels])
    plan, *others = parts_of(plan, CI, low - SEP, False, own[levels])
    for n in range(levels - 2):
        own[n + 1], sent[n + 1] = others[2 * n : 2 * n + 2]
    inner = []
    for step in range(levels):
        for level in range(levels, step, -1):
            exchange(level, step if level == levels else level - 1 - step)
            if level > step + 1:
                add(level, x_vmem, rhs_vmem, *inner, *[array for n, array in own.items() if n != level])
            if (level, step) == (levels, 0):
                plan, *inner = parts_of(plan, 0, CI, False, sent[levels])

    sums = [array for level in range(1, levels - 1) for array in (own[level], got[level])]
    alive = [sent[levels], own[levels], own[levels - 1]]
    terms, plan = pl.pallas_call(
        functools.partial(lower_kernel, per, levels - 2),
        out_shape=(tiles(row_blocks + 1, F32), plan_out),
        in_specs=[SMEM] + [VMEM] * (2 + len(sums) + len(alive)),
        out_specs=(VMEM, SMEM),
        scratch_shapes=[tiles(low - SEP, BF16)],
        input_output_aliases={0: 1},
        compiler_params=params,
        cost_estimate=free,
    )(plan, *in_vmem(x_vmem, *inner, *sums, *alive))

    second = levels - 1
    terms = pl.pallas_call(
        functools.partial(mid_kernel, per, low - SEP),
        out_shape=tiles(row_blocks + 1, F32),
        in_specs=[SMEM] + [VMEM] * 4,
        out_specs=VMEM,
        scratch_shapes=[tiles(SEP, BF16)],
        input_output_aliases={4: 0},
        compiler_params=params,
        cost_estimate=free,
    )(plan, *in_vmem(x_vmem, own[second], got[second], terms))

    part_shape = (n_col // 4, per, block, columns)
    parts = (pltpu.VMEM(part_shape, F32), pltpu.VMEM(part_shape, BF16))
    terms, coarse, far, far_send = pl.pallas_call(
        functools.partial(far_kernel, low, per),
        out_shape=(tiles(row_blocks + 1, F32), tiles(SEP, BF16), *parts),
        in_specs=[SMEM] + [VMEM] * 4,
        out_specs=(VMEM,) * 4,
        input_output_aliases={4: 0},
        compiler_params=params,
        cost_estimate=free,
    )(plan, *in_vmem(x_vmem, own[levels], got[levels], terms))
    _, near, near_send = pl.pallas_call(
        functools.partial(near_kernel, low, per),
        out_shape=(tiles(row_blocks + 1, F32), *parts),
        in_specs=[SMEM] + [VMEM] * 3,
        out_specs=(VMEM,) * 3,
        input_output_aliases={3: 0},
        compiler_params=params,
        cost_estimate=free,
    )(plan, *in_vmem(x_vmem, coarse, terms))

    def reduce_low_bits(keep, send):
        bit = 1
        while True:
            keep = keep + swap(send, "col", bit).astype(F32)
            bit *= 2
            if bit == n_col // 2:
                return keep[0]
            pairs = keep.reshape(-1, 2, per, block, columns)
            keep, send = pairs[:, 0], pairs[:, 1].astype(BF16)

    far = reduce_low_bits(far, far_send).astype(BF16)
    total = reduce_low_bits(near, near_send) + swap(far, "col", n_col // 2).astype(F32)
    return total.reshape(per * block, columns).astype(BF16)


def solution(mesh):
    in_specs = (
        P("leaf", None),
        P("leaf", "col", None, None, None),
        P("leaf", "col", None),
        P("leaf", "col", None),
        P("leaf", "col"),
    )
    out_specs = P(("leaf", "col"), None)
    return jax.shard_map(body, mesh=mesh, in_specs=in_specs, out_specs=out_specs, check_vma=False)
```

```python
import functools

import jax
import jax.numpy as jnp
from jax import lax
from jax.experimental import pallas as pl
from jax.experimental.pallas import tpu as pltpu
from jax.sharding import PartitionSpec as P

CI = 2
SEP = 2
LARGE, SMALL = 32, 16
CHUNKS = 4
BITS = 10
VMEM_LIMIT = 8 << 20

F32 = jnp.float32
BF16 = jnp.bfloat16
VMEM = pl.BlockSpec(memory_space=pltpu.VMEM)
SMEM = pl.BlockSpec(memory_space=pltpu.SMEM)
ANY = pl.BlockSpec(memory_space=pl.ANY)
ALL, TOP, REST, FAR, NEAR, SIZES, PLAN_ROWS = 0, 1, 2, 3, 4, 5, 8


def swap(x, axis, bits):
    return lax.ppermute(x, axis, [(i, i ^ bits) for i in range(lax.axis_size(axis))])


def over_list(plan_ref, which, begin, end, one):
    mask = (1 << BITS) - 1

    def body(size):
        def group(j, base):
            for u in range(size):
                at = base + u
                entry = plan_ref[which, jnp.minimum(at, end - 1)]
                one(entry & mask, (entry >> BITS) & mask, entry >> (2 * BITS), at < end)
            return base + size

        return group

    base = lax.fori_loop(0, (end - begin + LARGE - SMALL - 1) // LARGE, body(LARGE), begin)
    lax.fori_loop(0, (end - base + SMALL - 1) // SMALL, body(SMALL), base)


def project(which, begin, end, low, plan_ref, x_ref, rhs_ref, acc_ref):
    block = x_ref.shape[1]
    trash = acc_ref.shape[0] - 1

    def one(k, row, col, used):
        at = pl.multiple_of(row * block, block)
        acc_ref[jnp.where(used, col - low, trash)] += lax.dot_general(
            x_ref[k], rhs_ref[pl.ds(at, block), :], (((0,), (0,)), ((), ())), preferred_element_type=F32
        )

    over_list(plan_ref, which, begin, end, one)


def image(which, begin, end, low, per, flip, plan_ref, x_ref, coarse_ref, acc_ref):
    trash = acc_ref.shape[0] - 1

    def one(k, row, col, used):
        at = ((row // per) ^ flip) * per + row % per
        acc_ref[jnp.where(used, at, trash)] += jnp.dot(x_ref[k], coarse_ref[col - low], preferred_element_type=F32)

    over_list(plan_ref, which, begin, end, one)


def list_slots(plan_ref, found, low, high, list_len):
    def scan(j, found):
        for u in range(8):
            entry = plan_ref[ALL, j * 8 + u]
            plan_ref[REST, found] = entry
            col = entry >> (2 * BITS)
            found += ((col >= low) & (col < high)).astype(jnp.int32)
        return found

    return lax.fori_loop(0, list_len // 8, scan, found)


def first_kernel(low, high, x_hbm, rhs_hbm, row_hbm, col_hbm, count_hbm, x_ref, rhs_ref, part_ref, half_ref, plan_ref,
                 row_ref, col_ref, count_ref, acc_ref, id_sem, big_sem):
    list_len = x_ref.shape[0]
    chunk = list_len // CHUNKS
    ids = [
        pltpu.make_async_copy(row_hbm, row_ref, id_sem.at[0]),
        pltpu.make_async_copy(col_hbm, col_ref, id_sem.at[1]),
        pltpu.make_async_copy(count_hbm, count_ref, id_sem.at[2]),
    ]
    big = [pltpu.make_async_copy(rhs_hbm, rhs_ref, big_sem.at[CHUNKS])]
    for i in range(CHUNKS):
        at = pl.ds(i * chunk, chunk)
        big.append(pltpu.make_async_copy(x_hbm.at[at], x_ref.at[at], big_sem.at[i]))
    for copy in ids + big:
        copy.start()
    acc_ref[...] = jnp.zeros_like(acc_ref)
    for copy in ids:
        copy.wait()
    count = count_ref[0]

    def scan(j, carry):
        found, second = carry
        for u in range(8):
            k = j * 8 + u
            col = jnp.where(k < count, col_ref[k], high)
            entry = k + (row_ref[k] << BITS) + (col << (2 * BITS))
            plan_ref[ALL, k] = entry
            plan_ref[TOP, found] = entry
            plan_ref[REST, second] = entry
            found += ((col >= low) & (col < high)).astype(jnp.int32)
            second += ((col >= low - SEP) & (col < low)).astype(jnp.int32)
        return found, second

    found, second = lax.fori_loop(0, list_len // 8, scan, (jnp.int32(0), jnp.int32(0)))
    plan_ref[SIZES, TOP] = found
    plan_ref[SIZES, REST] = second
    for copy in big:
        copy.wait()
    project(TOP, jnp.int32(0), found, low, plan_ref, x_ref, rhs_ref, acc_ref)
    for c in range(high - low):
        part_ref[c] = acc_ref[c]
        half_ref[c] = acc_ref[c].astype(BF16)


def part_kernel(low, high, second, old_plan_ref, x_ref, rhs_ref, _, plan_ref, *refs):
    outs, acc_ref = refs[:-1], refs[-1]
    acc_ref[...] = jnp.zeros_like(acc_ref)
    begin, end = jnp.int32(0), plan_ref[SIZES, REST]
    if not second:
        begin = plan_ref[SIZES, ALL] if low == 0 else end
        end = list_slots(plan_ref, begin, low, high, x_ref.shape[0])
        plan_ref[SIZES, ALL] = end
    project(REST, begin, end, low, plan_ref, x_ref, rhs_ref, acc_ref)
    if low == 0:
        for c in range(CI):
            outs[0][c] = acc_ref[c].astype(BF16)
    for n in range(len(outs) // 2):
        part_ref, half_ref = outs[2 * n : 2 * n + 2]
        for c in range(SEP):
            part_ref[c] = acc_ref[n * SEP + c]
            half_ref[c] = acc_ref[n * SEP + c].astype(BF16)


def add_kernel(own_ref, got_ref, *refs):
    sum_ref, half_ref = refs[-2:]
    total = own_ref[...] + got_ref[...].astype(F32)
    sum_ref[...] = total
    half_ref[...] = total.astype(BF16)


def sum_coarse(sums, coarse_ref, at):
    for n in range(len(sums) // 2):
        own_ref, got_ref = sums[2 * n : 2 * n + 2]
        coarse_ref[at + n * SEP : at + (n + 1) * SEP] = (own_ref[...] + got_ref[...].astype(F32)).astype(BF16)


def lower_kernel(per, levels, old_plan_ref, x_ref, inner_ref, *refs):
    acc_ref, plan_ref, coarse_ref = refs[-3:]
    acc_ref[...] = jnp.zeros_like(acc_ref)
    coarse_ref[:CI] = inner_ref[...]
    sum_coarse(refs[: 2 * levels], coarse_ref, CI)
    me = lax.axis_index("col")
    half = (acc_ref.shape[0] - 1) // per // 2

    def scan(j, found):
        far, near = found
        entry = plan_ref[TOP, j]
        plan_ref[FAR, far] = entry
        plan_ref[NEAR, near] = entry
        is_far = (((((entry >> BITS) & ((1 << BITS) - 1)) // per) ^ me) >= half).astype(jnp.int32)
        return far + is_far, near + 1 - is_far

    far, near = lax.fori_loop(0, plan_ref[SIZES, TOP], scan, (jnp.int32(0), jnp.int32(0)))
    plan_ref[SIZES, FAR] = far
    plan_ref[SIZES, NEAR] = near
    image(REST, plan_ref[SIZES, REST], plan_ref[SIZES, ALL], 0, per, me, plan_ref, x_ref, coarse_ref, acc_ref)


def mid_kernel(per, low, plan_ref, x_ref, own_ref, got_ref, old_ref, acc_ref, coarse_ref):
    sum_coarse((own_ref, got_ref), coarse_ref, 0)
    image(REST, jnp.int32(0), plan_ref[SIZES, REST], low, per, lax.axis_index("col"), plan_ref, x_ref, coarse_ref, acc_ref)


def split(half, per, acc_ref, keep_ref, send_ref):
    for g in range(keep_ref.shape[0]):
        for b in range(per):
            send_ref[g, b] = acc_ref[half + (2 * g + 1) * per + b].astype(BF16)
            keep_ref[g, b] = acc_ref[half + 2 * g * per + b]


def far_kernel(low, per, plan_ref, x_ref, own_ref, got_ref, old_ref, acc_ref, coarse_ref, keep_ref, send_ref):
    coarse_ref[...] = (own_ref[...] + got_ref[...].astype(F32)).astype(BF16)
    image(FAR, jnp.int32(0), plan_ref[SIZES, FAR], low, per, lax.axis_index("col"), plan_ref, x_ref, coarse_ref, acc_ref)
    split((acc_ref.shape[0] - 1) // 2, per, acc_ref, keep_ref, send_ref)


def near_kernel(low, per, plan_ref, x_ref, coarse_ref, old_ref, acc_ref, keep_ref, send_ref):
    image(NEAR, jnp.int32(0), plan_ref[SIZES, NEAR], low, per, lax.axis_index("col"), plan_ref, x_ref, coarse_ref, acc_ref)
    split(0, per, acc_ref, keep_ref, send_ref)


def body(right_side, x_blocks, row_ids, col_ids, counts):
    blocks, rows, cols, count = x_blocks[0, 0], row_ids[0, 0], col_ids[0, 0], counts[0]
    list_len, block, _ = blocks.shape
    columns = right_side.shape[1]
    row_blocks = right_side.shape[0] // block
    levels = lax.axis_size("leaf").bit_length() - 1
    n_col = lax.axis_size("col")
    per = row_blocks // n_col
    slots = CI + levels * SEP
    low = slots - SEP
    params = pltpu.CompilerParams(vmem_limit_bytes=VMEM_LIMIT)
    free = pl.CostEstimate(flops=0, bytes_accessed=0, transcendentals=0)

    def tiles(n, dtype):
        return pltpu.VMEM((n, block, columns), dtype)

    def in_vmem(*arrays):
        return [pltpu.with_memory_space_constraint(a, pltpu.VMEM) for a in arrays]

    def in_hbm(*arrays):
        return [pltpu.with_memory_space_constraint(a, pltpu.HBM) for a in arrays]

    plan_shape = (PLAN_ROWS, (list_len + 128) // 128 * 128)
    plan_out = pltpu.SMEM(plan_shape, jnp.int32)
    pair = (tiles(SEP, F32), tiles(SEP, BF16))
    sem = pltpu.SemaphoreType.DMA

    x_vmem, rhs_vmem, part, half, plan = pl.pallas_call(
        functools.partial(first_kernel, low, slots),
        out_shape=(pltpu.VMEM(blocks.shape, BF16), pltpu.VMEM(right_side.shape, BF16), *pair, plan_out),
        in_specs=[ANY] * 5,
        out_specs=(*(VMEM,) * 4, SMEM),
        scratch_shapes=[
            pltpu.SMEM((list_len,), jnp.int32),
            pltpu.SMEM((list_len,), jnp.int32),
            pltpu.SMEM((1,), jnp.int32),
            tiles(SEP + 1, F32),
            sem((3,)),
            sem((CHUNKS + 1,)),
        ],
        compiler_params=params,
        cost_estimate=free,
    )(*in_hbm(blocks, right_side, rows, cols), count)
    own, sent, got = {levels: part}, {levels: half}, {}

    def exchange(level, step):
        bits = (2 << step) - 2 if step > 1 else 1 << step
        got[level] = swap(sent[level], "leaf", bits)

    def add(level, *alive):
        own[level], sent[level] = pl.pallas_call(
            add_kernel,
            out_shape=pair,
            in_specs=[VMEM] * (2 + len(alive)),
            out_specs=(VMEM,) * 2,
            compiler_params=params,
            cost_estimate=free,
        )(*in_vmem(own[level], got[level], *alive))

    def parts_of(plan, low, high, second, after):
        pairs = (tiles(CI, BF16),) if low == 0 else pair * ((high - low) // SEP)
        return pl.pallas_call(
            functools.partial(part_kernel, low, high, second),
            out_shape=(plan_out, *pairs),
            in_specs=[SMEM, VMEM, VMEM, VMEM],
            out_specs=(SMEM, *(VMEM,) * len(pairs)),
            scratch_shapes=[tiles(high - low + 1, F32)],
            input_output_aliases={0: 0},
            compiler_params=params,
            cost_estimate=free,
        )(plan, *in_vmem(x_vmem, rhs_vmem, after))

    plan, own[levels - 1], sent[levels - 1] = parts_of(plan, low - SEP, low, True, own[levels])
    plan, *others = parts_of(plan, CI, low - SEP, False, own[levels])
    for n in range(levels - 2):
        own[n + 1], sent[n + 1] = others[2 * n : 2 * n + 2]
    inner = []
    for step in range(levels):
        for level in range(levels, step, -1):
            exchange(level, step if level == levels else level - 1 - step)
            if level > step + 1:
                add(level, x_vmem, rhs_vmem, *inner, *[array for n, array in own.items() if n != level])
            if (level, step) == (levels, 0):
                plan, *inner = parts_of(plan, 0, CI, False, sent[levels])

    sums = [array for level in range(1, levels - 1) for array in (own[level], got[level])]
    alive = [sent[levels], own[levels], own[levels - 1]]
    terms, plan = pl.pallas_call(
        functools.partial(lower_kernel, per, levels - 2),
        out_shape=(tiles(row_blocks + 1, F32), plan_out),
        in_specs=[SMEM] + [VMEM] * (2 + len(sums) + len(alive)),
        out_specs=(VMEM, SMEM),
        scratch_shapes=[tiles(low - SEP, BF16)],
        input_output_aliases={0: 1},
        compiler_params=params,
        cost_estimate=free,
    )(plan, *in_vmem(x_vmem, *inner, *sums, *alive))

    second = levels - 1
    terms = pl.pallas_call(
        functools.partial(mid_kernel, per, low - SEP),
        out_shape=tiles(row_blocks + 1, F32),
        in_specs=[SMEM] + [VMEM] * 4,
        out_specs=VMEM,
        scratch_shapes=[tiles(SEP, BF16)],
        input_output_aliases={4: 0},
        compiler_params=params,
        cost_estimate=free,
    )(plan, *in_vmem(x_vmem, own[second], got[second], terms))

    part_shape = (n_col // 4, per, block, columns)
    parts = (pltpu.VMEM(part_shape, F32), pltpu.VMEM(part_shape, BF16))
    terms, coarse, far, far_send = pl.pallas_call(
        functools.partial(far_kernel, low, per),
        out_shape=(tiles(row_blocks + 1, F32), tiles(SEP, BF16), *parts),
        in_specs=[SMEM] + [VMEM] * 4,
        out_specs=(VMEM,) * 4,
        input_output_aliases={4: 0},
        compiler_params=params,
        cost_estimate=free,
    )(plan, *in_vmem(x_vmem, own[levels], got[levels], terms))
    _, near, near_send = pl.pallas_call(
        functools.partial(near_kernel, low, per),
        out_shape=(tiles(row_blocks + 1, F32), *parts),
        in_specs=[SMEM] + [VMEM] * 3,
        out_specs=(VMEM,) * 3,
        input_output_aliases={3: 0},
        compiler_params=params,
        cost_estimate=free,
    )(plan, *in_vmem(x_vmem, coarse, terms))

    def reduce_low_bits(keep, send):
        bit = 1
        while True:
            keep = keep + swap(send, "col", bit).astype(F32)
            bit *= 2
            if bit == n_col // 2:
                return keep[0]
            pairs = keep.reshape(-1, 2, per, block, columns)
            keep, send = pairs[:, 0], pairs[:, 1].astype(BF16)

    far = reduce_low_bits(far, far_send).astype(BF16)
    total = reduce_low_bits(near, near_send) + swap(far, "col", n_col // 2).astype(F32)
    return total.reshape(per * block, columns).astype(BF16)


def solution(mesh):
    in_specs = (
        P("leaf", None),
        P("leaf", "col", None, None, None),
        P("leaf", "col", None),
        P("leaf", "col", None),
        P("leaf", "col"),
    )
    out_specs = P(("leaf", "col"), None)
    return jax.shard_map(body, mesh=mesh, in_specs=in_specs, out_specs=out_specs, check_vma=False)
```
